32 devices in a mesh: section: 2 (over x), expert: 4 (over z), dp: 4 (over y, core).
Axes of the slice: x: 2, y: 2, z: 4, core: 2. Of those that a mesh axis runs over, the one named last changes fastest.
Arguments:
- fresh_tokens: bfloat16 [2, 1024, 4096], P(None, ('expert', 'dp')), may hold values from -60 to 60
- in_flight: bfloat16 [1024, 4096], P(('expert', 'dp')), may hold values from -60 to 60
- norm_weight: float32 [2, 4096], P('section'), may hold values from 0.1 to 1.9
- gate_up: bfloat16 [2, 16, 2, 4096, 768], P('section', 'expert', None, 'dp'), may hold values from -0.09375 to 0.09375
- down_proj: bfloat16 [2, 16, 768, 4096], P('section', 'expert', 'dp'), may hold values from -0.21875 to 0.21875
- first_moment: bfloat16 [2, 16, 768, 4096], P('section', 'expert', 'dp'), may hold values from -6 to 6
- second_moment: bfloat16 [2, 16, 768, 4096], P('section', 'expert', 'dp'), may hold values from 0.099609375 to 4
- route_ids: int32 [2, 2, 1024, 8], P('section', None, ('expert', 'dp')), may hold values from 0 to 15, all different within a row; in each aligned block of 64 rows (0 to 63, 64 to 127, ..., all dimensions but the last counted through in order) at most 36 rows name the same one
- route_probs: float32 [2, 2, 1024, 8], P('section', None, ('expert', 'dp')), may hold values from 0.05 to 1
- trade_flags: int32 [2, 4], replicated, may hold values from 0 to 1, as said below
Outputs:
- layer_out: bfloat16 [2, 2, 1024, 4096], P('section', None, ('expert', 'dp'))
- gate_up_moved: bfloat16 [2, 16, 2, 4096, 768], P('section', 'expert', None, 'dp')
- down_moved: bfloat16 [2, 16, 768, 4096], P('section', 'expert', 'dp')
- first_moved: bfloat16 [2, 16, 768, 4096], P('section', 'expert', 'dp')
- second_moved: bfloat16 [2, 16, 768, 4096], P('section', 'expert', 'dp')
The draws below stay inside these ranges and needn't reach their ends.
Inputs may be any that keep to these rules, and one draw needn't show every extreme that they name: `route_ids`: in each aligned block of 64 rows (one device's tokens of one section and tick) the 8 experts of a token differ and no expert is chosen by more than 36 rows. `trade_flags`: at least one entry is 1 and at least one is 0.
All inputs are finite; a program needn't handle non-finite values.
Results may differ from the reference program's by a relative error of at most 0.0035.
Values may be sent and summed in bfloat16 or wider, within the bound.
No kernel may reach another device: no remote copies, remote signals or barrier semaphores. Data moves between devices by JAX's collectives and lax.ppermute only.
A program may use at most 256 MiB of HBM per device.

```python
import math
import jax
import jax.numpy as jnp
import numpy as np
from jax import lax

D = 4096
FF = 768
EXPERTS = 16
TOPK = 8
TICKS = 2
TOK_DEV = 64
SECTIONS = 2
EXP_DEV = 4
CAP = 36
TOKENS = 1024
PAIRS = 2
N_EXPERT = 4
N_DP = 4


def scaled_rows(key, shape):
    key_value, key_row, key_col = jax.random.split(key, 3)
    values = jax.random.normal(key_value, shape, jnp.float32)
    row_scale = jnp.exp(jax.random.uniform(key_row, shape[:-1] + (1,), jnp.float32, -1.15, 1.15))
    col_scale = jnp.exp(jax.random.uniform(key_col, (shape[-1],), jnp.float32, -1.15, 1.15))
    return jnp.clip(values * row_scale * col_scale, -60.0, 60.0)


def draw_fresh_tokens(key, part):
    return scaled_rows(jax.random.fold_in(key, 11), (TICKS, TOKENS, D)).astype(jnp.bfloat16)


def draw_in_flight(key, part):
    return scaled_rows(jax.random.fold_in(key, 23), (TOKENS, D)).astype(jnp.bfloat16)


def draw_trade_flags(key, part):
    key_perm, key_count = jax.random.split(jax.random.fold_in(key, 37))
    entries = PAIRS * EXP_DEV
    ordering = jax.random.permutation(key_perm, entries)
    how_many = jax.random.randint(key_count, (), 1, entries)
    return (ordering < how_many).astype(jnp.int32).reshape(PAIRS, EXP_DEV)


def block_levels(own_key, extent, cuts, low, top_value):
    def one(position, parts):
        steps = jax.random.uniform(jax.random.fold_in(jax.random.fold_in(own_key, 6), position), (parts,), jnp.float32, low / len(cuts), top_value / len(cuts))
        return jnp.repeat(jnp.exp(steps), extent[position] // parts).reshape((-1,) + (1,) * (len(extent) - position - 1))

    factor_of = one(*cuts[0])
    for cut in cuts[1:]:
        factor_of = factor_of * one(*cut)
    return factor_of


def deal_out(own_key, own, number, rows, amount, top, bound, skew):
    ranking = jax.random.permutation(own_key, amount)
    crowded, ordinary = portions_of(amount, rows * top, bound, skew, True), portions_of(amount, rows * top, bound, skew, False)
    places = jnp.arange(amount)

    def named(sizes, offset_by):
        used = int((sizes > 0).sum())
        fixed = max(1, used // 4)
        moved = fixed + (places - fixed + offset_by * (used - fixed)) % max(1, amount - fixed)
        return jnp.zeros((amount,), jnp.int32).at[ranking[jnp.where(places < fixed, places, moved)]].set(jnp.asarray(sizes, jnp.int32))

    sizes = jnp.where(number % 4 == 0, named(crowded, number // 4), named(ordinary, number - number // 4 - 1))
    mixed = jax.random.permutation(jax.random.fold_in(own, 3), amount)
    source_of, sink = mixed[0:amount // 2 * 2:2], mixed[1:amount // 2 * 2:2]
    room = jnp.minimum(sizes[source_of] - 1, bound - sizes[sink]) // 2
    room = jnp.where((source_of == ranking[0]) | (sink == ranking[0]) | (sizes[sink] == 0), 0, jnp.maximum(room, 0))
    moved = jax.random.randint(jax.random.fold_in(own, 4), (amount // 2,), 0, 1 << 20) % (room + 1)
    sizes = sizes.at[source_of].add(-moved).at[sink].add(moved)
    labels = jnp.searchsorted(jnp.cumsum(sizes), jnp.arange(rows * top), side="right").astype(jnp.int32)
    grid = labels.reshape(top, rows).T
    grid = grid[jax.random.permutation(jax.random.fold_in(own, 1), rows)]
    offset_by = jax.random.randint(jax.random.fold_in(own, 2), (rows, 1), 0, top)
    return jnp.take_along_axis(grid, (jnp.arange(top)[None, :] + offset_by) % top, axis=1)


def portions_of(count, total, most, slope, full):
    portions = [(1 << 20) // math.isqrt(grade ** slope) + 1 for grade in range(1, count + 1)]
    largest = most if full else min(most, max(-(-total // count), total * portions[0] // sum(portions)))
    least = 1 if total - largest >= count - 1 else 0
    given, rest = [largest] + [least] * (count - 1), total - largest - least * (count - 1)
    while rest > 0:
        movable = [i for i in range(1, count) if given[i] < largest] or [i for i in range(1, count) if given[i] < most]
        pool, budget = sum([portions[i] for i in movable]), rest
        for i in movable:
            addition = min(most - given[i], max(1, budget * portions[i] // pool), rest)
            given[i] = given[i] + addition
            rest = rest - addition
    return np.array(given)


def centred(rng, extent, spread, limit, cuts=(), kind=jnp.bfloat16):
    values = spread * jax.random.normal(rng, extent, jnp.float32)
    if cuts:
        values = values * block_levels(rng, extent, cuts, -0.22, 0.18)
    return jnp.clip(values, -limit, limit).astype(kind)


def setup_inputs(seed: int = 0) -> dict:
    seeds = jax.random.split(jax.random.key(seed), 11)
    fresh_tokens = draw_fresh_tokens(jax.random.fold_in(seeds[10], 71), 0)
    in_flight = draw_in_flight(jax.random.fold_in(seeds[10], 71), 0)
    norm_weight = jnp.clip(1.0 + 0.18 * jax.random.normal(seeds[2], (SECTIONS, D), jnp.float32), 0.1, 1.9)
    gate_up = centred(seeds[3], (SECTIONS, EXPERTS, 2, D, FF), D ** -0.5, 0.09375, ((0, 2), (1, 4), (3, 4)))
    down_proj = centred(seeds[4], (SECTIONS, EXPERTS, FF, D), FF ** -0.5, 0.21875, ((0, 2), (1, 4), (2, 4)))
    first_moment = centred(seeds[5], (SECTIONS, EXPERTS, FF, D), 1.0, 6.0, ((0, 2), (1, 4), (2, 4)))
    second_moment = jnp.clip(jnp.exp(math.log(4.0) - 3.6927934 * jax.random.uniform(seeds[6], (SECTIONS, EXPERTS, FF, D), jnp.float32) ** block_levels(seeds[6], (SECTIONS, EXPERTS, FF, D), ((0, 2), (1, 4), (2, 4)), -0.2, 0.2)), 0.099609375, 4.0).astype(jnp.bfloat16)
    route_ids_keys = jax.random.split(jax.random.fold_in(seeds[7], 1), SECTIONS * TICKS * TOKENS // TOK_DEV)
    route_ids_turns = jax.random.permutation(jax.random.fold_in(seeds[7], 3), SECTIONS * TICKS * TOKENS // TOK_DEV)
    route_ids = jax.vmap(lambda own, number: deal_out(jax.random.fold_in(seeds[7], 2), own, number, TOK_DEV, EXPERTS, TOPK, CAP, 2))(route_ids_keys, route_ids_turns).reshape((SECTIONS, TICKS, TOKENS, TOPK))
    route_probs = jnp.clip(jnp.exp(math.log(1.0) - 2.9957323 * jax.random.uniform(seeds[8], (SECTIONS, TICKS, TOKENS, TOPK), jnp.float32) ** block_levels(seeds[8], (SECTIONS, TICKS, TOKENS, TOPK), ((0, 2), (2, 16)), -0.2, 0.2)), 0.05, 1.0)
    trade_flags = draw_trade_flags(jax.random.fold_in(seeds[10], 71), 0)
    return dict(fresh_tokens=fresh_tokens, in_flight=in_flight, norm_weight=norm_weight, gate_up=gate_up, down_proj=down_proj, first_moment=first_moment, second_moment=second_moment, route_ids=route_ids, route_probs=route_probs, trade_flags=trade_flags)


def rms_normed(inputs, norm_gain):
    values = inputs.astype(jnp.float32)
    inverse_rms = lax.rsqrt(lax.optimization_barrier(jnp.mean(values * values, axis=-1, keepdims=True)) + 1e-06)
    return (values * inverse_rms * norm_gain).astype(jnp.bfloat16)

def moe_layer(inputs, norm_gain, section_gate_up, section_down, layer_ids, layer_probs):
    normed = rms_normed(inputs, norm_gain)
    mix_weight = layer_probs / lax.optimization_barrier(jnp.sum(layer_probs, axis=-1, keepdims=True))
    flat_ids = layer_ids.reshape(-1)
    flat_weight = mix_weight.reshape(-1)
    most_rows = N_EXPERT * N_DP * CAP
    token_count = normed.shape[0]

    def per_expert(running, expert):
        member = (flat_ids != expert).astype(jnp.int32)
        ordering = jnp.argsort(member, stable=True)[:most_rows].astype(jnp.int32)
        live_rows = member[ordering] == 0
        token_rows = (ordering // TOPK).astype(jnp.int32)
        rows_in = normed[token_rows]
        gate_part = jnp.dot(rows_in, section_gate_up[expert, 0], preferred_element_type=jnp.float32)
        up_part = jnp.dot(rows_in, section_gate_up[expert, 1], preferred_element_type=jnp.float32)
        active = (jax.nn.silu(gate_part) * up_part).astype(jnp.bfloat16)
        expert_out = jnp.dot(active, section_down[expert], preferred_element_type=jnp.float32).astype(jnp.bfloat16)
        scaled = jnp.where(live_rows, flat_weight[ordering], 0.0)[:, None] * expert_out.astype(jnp.float32)
        running = running + jax.ops.segment_sum(scaled, token_rows, num_segments=token_count)
        return (running, None)
    running, _ = lax.scan(per_expert, inputs.astype(jnp.float32), jnp.arange(EXPERTS, dtype=jnp.int32))
    return running.astype(jnp.bfloat16)

def reference(fresh_tokens, in_flight, norm_weight, gate_up, down_proj, first_moment, second_moment, route_ids, route_probs, trade_flags):
    section_rows = []
    for section_step in range(SECTIONS):
        tick_list = []
        for tick_step in range(TICKS):
            if section_step == 0:
                inputs = fresh_tokens[tick_step]
            elif tick_step == 0:
                inputs = in_flight
            else:
                inputs = section_rows[section_step - 1][tick_step - 1]
            tick_list.append(moe_layer(inputs, norm_weight[section_step], gate_up[section_step], down_proj[section_step], route_ids[section_step, tick_step], route_probs[section_step, tick_step]))
        section_rows.append(tick_list)
    layer_out = jnp.stack([jnp.stack(tick_list) for tick_list in section_rows])
    half_span = N_EXPERT // 2
    per_device = EXPERTS // N_EXPERT
    blocks = jnp.arange(N_EXPERT, dtype=jnp.int32)
    pair_flags = trade_flags[blocks % half_span]
    source = jnp.where(pair_flags == 1, (blocks ^ half_span)[:, None], blocks[:, None]).astype(jnp.int32)
    slot_grid = jnp.broadcast_to(jnp.arange(per_device, dtype=jnp.int32)[None, :], (N_EXPERT, per_device))

    def relocate(stacked):
        shaped = stacked.reshape((SECTIONS, N_EXPERT, per_device) + stacked.shape[2:])
        return shaped[:, source, slot_grid].reshape(stacked.shape)
    return (layer_out, relocate(gate_up), relocate(down_proj), relocate(first_moment), relocate(second_moment))
```

```python
import jax
import jax.numpy as jnp
from jax import lax
from jax.sharding import PartitionSpec as P

EXPERTS = 16
CAP = 36
COLUMN_PARTS = 4


def swap(value, axis, bit):
    return lax.ppermute(value, axis, [(i, i ^ (1 << bit)) for i in range(lax.axis_size(axis))])


def bits_of(axis):
    return lax.axis_size(axis).bit_length() - 1


def gather_relative(block, axis):
    held = block[None]
    for bit in reversed(range(bits_of(axis))):
        other = swap(held, axis, bit)
        held = jnp.stack([held, other], axis=1).reshape((-1,) + block.shape)
    return held


def scatter_relative(parts, axis):
    for bit in range(bits_of(axis)):
        paired = parts.reshape((parts.shape[0] // 2, 2) + parts.shape[1:])
        other = swap(paired[:, 1].astype(jnp.bfloat16), axis, bit)
        parts = paired[:, 0].astype(jnp.float32) + other.astype(jnp.float32)
    return parts[0]


def rms_normed(inputs, norm_gain):
    values = inputs.astype(jnp.float32)
    inverse_rms = lax.rsqrt(jnp.mean(values * values, axis=-1, keepdims=True) + 1e-06)
    return (values * inverse_rms * norm_gain).astype(jnp.bfloat16)


def exchange_slices(normed, dp_rank):
    ranks = lax.axis_size("dp")
    rows, width = normed.shape
    part = width // ranks
    columns = [
        lax.dynamic_slice_in_dim(normed, (dp_rank ^ r) * part, part, axis=1) for r in range(ranks)
    ]
    arrived = [columns[0]] + [
        lax.ppermute(columns[r], "dp", [(i, i ^ r) for i in range(ranks)]) for r in range(1, ranks)
    ]
    return jnp.concatenate(arrived, axis=0)


def route_tables(layer_ids, layer_probs):
    mix_weight = layer_probs / jnp.sum(layer_probs, axis=-1, keepdims=True)
    chosen = layer_ids[..., None] == jnp.arange(EXPERTS, dtype=jnp.int32)
    weights = jnp.sum(jnp.where(chosen, mix_weight[..., None], 0.0), axis=-2)
    member = jnp.any(chosen, axis=-2)
    rank = jnp.cumsum(member.astype(jnp.float32), axis=-2) - 1.0
    return weights, jnp.where(member, rank, -1.0)


def per_device(
    fresh_tokens,
    in_flight,
    norm_weight,
    gate_up,
    down_proj,
    first_moment,
    second_moment,
    route_ids,
    route_probs,
    trade_flags,
):
    groups = lax.axis_size("expert")
    dp_ranks = lax.axis_size("dp")
    half_span = groups // 2
    top_bit = bits_of("expert") - 1
    own_rank = lax.axis_index("expert")
    dp_rank = lax.axis_index("dp")
    section_index = lax.axis_index("section")
    experts_here = gate_up.shape[1]
    hidden = down_proj.shape[2]
    width = fresh_tokens.shape[2]
    block = fresh_tokens.shape[1]

    holdings = (gate_up, down_proj, first_moment, second_moment)
    counts = jnp.sum(trade_flags, axis=1)
    order = jnp.argsort(-trade_flags, axis=1, stable=True).astype(jnp.int32)
    own_pair = own_rank % half_span
    own_order = order[own_pair]
    own_count = counts[own_pair]

    def pair_route(pairs):
        return [(i, i ^ (1 << top_bit)) for i in range(groups) if i % half_span in pairs]

    def trade_round(moved, turn, pairs, beside_layers=False):
        slot = own_order[turn]
        active = turn < own_count
        if len(pairs) < half_span:
            active = jnp.logical_and(active, own_pair == pairs[0])
        sent = [lax.dynamic_slice_in_dim(array, slot, 1, axis=1) for array in holdings]
        if beside_layers:
            ranks = [[i, i + half_span] for i in range(half_span)]
            both = [lax.all_gather(array, "expert", axis_index_groups=ranks) for array in sent]
            other = 1 - own_rank // half_span
            arrived = [lax.dynamic_index_in_dim(array, other, 0, keepdims=False) for array in both]
        else:
            arrived = [lax.ppermute(array, "expert", pair_route(pairs)) for array in sent]
        return tuple(
            lax.dynamic_update_slice_in_dim(old, jnp.where(active, new, own), slot, axis=1)
            for old, new, own in zip(moved, arrived, sent)
        )

    moved = trade_round(holdings, jnp.int32(0), tuple(range(half_span)), beside_layers=True)

    def columns_for(relative):
        piece = lax.dynamic_slice_in_dim(gate_up[0], (dp_rank ^ relative) * hidden, hidden, axis=3)
        return jnp.concatenate([piece[:, 0], piece[:, 1]], axis=-1)

    pieces = [columns_for(r) for r in range(dp_ranks)]
    down_flat = down_proj[0].reshape(experts_here * hidden, width)

    weights, places = route_tables(route_ids[0], route_probs[0])
    table = jnp.stack([weights, places])
    gathered = lax.all_gather(table, ("expert", "dp"), axis=0, tiled=False)
    gathered = gathered.reshape((groups, dp_ranks) + table.shape)
    gathered = gathered[own_rank ^ jnp.arange(groups)][:, dp_rank ^ jnp.arange(dp_ranks)]
    mine = lax.dynamic_slice_in_dim(gathered, own_rank * experts_here, experts_here, axis=5)
    mix = mine[:, :, 0]
    place = mine[:, :, 1]
    group_rows = dp_ranks * CAP

    def layer(inputs, tick, after_columns):
        normed = rms_normed(inputs, norm_weight[0])
        tokens = gather_relative(exchange_slices(normed, dp_rank), "expert")
        tick_mix = mix[:, :, tick].reshape(groups, dp_ranks * block, experts_here)
        offset = ((dp_rank ^ jnp.arange(dp_ranks)) * CAP).astype(jnp.float32)[None, :, None, None]
        tick_place = place[:, :, tick]
        tick_place = jnp.where(tick_place >= 0, tick_place + offset, -1.0)
        tick_place = tick_place.reshape(groups, dp_ranks * block, experts_here)
        row_number = jnp.arange(group_rows, dtype=jnp.float32)[None, :, None]
        folded = []
        for expert in range(experts_here):
            pick = (tick_place[:, None, :, expert] == row_number).astype(jnp.bfloat16)
            rows = jnp.einsum(
                "grt,gtd->grd", pick, tokens, preferred_element_type=jnp.float32
            ).astype(jnp.bfloat16)
            rows = rows.reshape(groups * group_rows, -1)
            products = jnp.stack(
                [
                    jnp.dot(rows, piece[expert], preferred_element_type=jnp.float32)
                    for piece in pieces
                ]
            )
            total = scatter_relative(products, "dp")
            active = jax.nn.silu(total[:, :hidden]) * total[:, hidden:]
            active = active.astype(jnp.bfloat16).reshape(groups, group_rows, hidden)
            spread = jnp.einsum(
                "grt,grf->gtf", pick, active, preferred_element_type=jnp.float32
            )
            folded.append((spread * tick_mix[:, :, expert, None]).astype(jnp.bfloat16))
        folded = jnp.concatenate(folded, axis=-1).reshape(-1, experts_here * hidden)
        part = width // COLUMN_PARTS
        results, extras = [], []
        for index in range(COLUMN_PARTS):
            columns = slice(index * part, (index + 1) * part)
            product = jnp.dot(folded, down_flat[:, columns], preferred_element_type=jnp.float32)
            product = product.reshape(groups, dp_ranks, block, part)
            product = jnp.swapaxes(product, 0, 1)
            combined = scatter_relative(scatter_relative(product, "dp"), "expert")
            result = (inputs[:, columns].astype(jnp.float32) + combined).astype(jnp.bfloat16)
            results.append(result)
            extras.append(after_columns(result))
        return jnp.concatenate(results, axis=1), extras

    sections = lax.axis_size("section")
    onward = [(i, i + 1) for i in range(sections - 1)]
    first_input = jnp.where(section_index == 0, fresh_tokens[0], in_flight)
    tick_zero, arrived = layer(first_input, 0, lambda x: lax.ppermute(x, "section", onward))
    arrived = jnp.concatenate(arrived, axis=1)
    second_input = jnp.where(section_index == 0, fresh_tokens[1], arrived)
    tick_one, _ = layer(second_input, 1, lambda x: None)
    layer_out = jnp.stack([tick_zero, tick_one])[None]

    if experts_here > 1:
        moved, layer_out = lax.optimization_barrier((moved, layer_out))
        fewest = jnp.min(counts)
        everyone = tuple(range(half_span))
        moved = lax.fori_loop(
            1, fewest, lambda turn, held: trade_round(held, turn, everyone), moved
        )
        start = jnp.maximum(fewest, 1)
        for pair in range(half_span):
            moved = lax.fori_loop(
                start,
                counts[pair],
                lambda turn, held, pair=pair: trade_round(held, turn, (pair,)),
                moved,
            )
    return (layer_out,) + tuple(moved)


def solution(mesh):
    return jax.shard_map(
        per_device,
        mesh=mesh,
        in_specs=(
            P(None, ("expert", "dp"), None),
            P(("expert", "dp"), None),
            P("section", None),
            P("section", "expert", None, "dp", None),
            P("section", "expert", "dp", None),
            P("section", "expert", "dp", None),
            P("section", "expert", "dp", None),
            P("section", None, ("expert", "dp"), None),
            P("section", None, ("expert", "dp"), None),
            P(),
        ),
        out_specs=(
            P("section", None, ("expert", "dp"), None),
            P("section", "expert", None, "dp", None),
            P("section", "expert", "dp", None),
            P("section", "expert", "dp", None),
            P("section", "expert", "dp", None),
        ),
        check_vma=False,
    )
```

```python
import functools

import jax
import jax.numpy as jnp
from jax import lax
from jax.experimental import pallas as pl
from jax.experimental.pallas import tpu as pltpu
from jax.sharding import PartitionSpec as P

EXPERTS = 16
CAP = 36
LANES = 128
VMEM_LIMIT = 24 * 1024 * 1024
SMEM = pl.BlockSpec(memory_space=pltpu.SMEM)


def swap(value, axis, bit):
    return lax.ppermute(value, axis, [(i, i ^ (1 << bit)) for i in range(lax.axis_size(axis))])


def bits_of(axis):
    return lax.axis_size(axis).bit_length() - 1


def reversed_order(count):
    if count == 1:
        return [0]
    return [2 * i for i in reversed_order(count // 2)] + [2 * i + 1 for i in reversed_order(count // 2)]


def call(kernel, name, flops, bytes_accessed, **options):
    return pl.pallas_call(
        kernel,
        name=name,
        cost_estimate=pl.CostEstimate(
            flops=flops, bytes_accessed=bytes_accessed, transcendentals=0
        ),
        compiler_params=pltpu.CompilerParams(vmem_limit_bytes=VMEM_LIMIT),
        **options,
    )


def arrange_kernel(ranks, hidden, place_ref, gate_up_ref, kept_ref, sent_ref):
    half = ranks // 2
    for rank in range(ranks):

        @pl.when(place_ref[0] == rank)
        def _():
            for position, relative in enumerate(reversed_order(ranks)):
                out_ref = kept_ref if position < half else sent_ref
                start = (position % half) * 2 * hidden
                columns = pl.ds((rank ^ relative) * hidden, hidden)
                out_ref[0, :, start : start + 2 * hidden] = jnp.concatenate(
                    [gate_up_ref[0, 0, 0, :, columns], gate_up_ref[0, 0, 1, :, columns]], axis=-1
                )


def arrange_weights(place, gate_up, ranks, hidden):
    _, experts, _, depth, columns = gate_up.shape
    tile = min(depth, 256)
    shape = jax.ShapeDtypeStruct((experts, depth, columns), jnp.bfloat16)
    spec = pl.BlockSpec((1, tile, columns), lambda e, d: (e, d, 0))
    return call(
        functools.partial(arrange_kernel, ranks, hidden),
        "arrange_weights",
        0,
        4 * gate_up.size,
        grid=(experts, depth // tile),
        in_specs=[SMEM, pl.BlockSpec((1, 1, 2, tile, columns), lambda e, d: (0, e, 0, d, 0))],
        out_specs=[spec, spec],
        out_shape=[shape, shape],
    )(place, gate_up)


def prepare_kernel(ranks, place_ref, inputs_ref, gain_ref, ids_ref, probs_ref, out_ref, normed_ref):
    rows, width = inputs_ref.shape
    part = width // ranks
    values = inputs_ref[...].astype(jnp.float32)
    inverse_rms = lax.rsqrt(jnp.mean(values * values, axis=-1, keepdims=True) + 1e-06)
    normed_ref[...] = (values * inverse_rms * gain_ref[...]).astype(jnp.bfloat16)

    probs = probs_ref[...]
    mix_weight = probs / jnp.sum(probs, axis=-1, keepdims=True)
    lane = lax.broadcasted_iota(jnp.int32, (rows, LANES), 1)
    field = lax.div(lane, EXPERTS)
    expert = lane - field * EXPERTS
    weights = jnp.zeros((rows, LANES), jnp.float32)
    member = jnp.zeros((rows, LANES), jnp.float32)
    for choice in range(probs.shape[1]):
        hit = ids_ref[:, choice : choice + 1] == expert
        weights = weights + jnp.where(hit, mix_weight[:, choice : choice + 1], 0.0)
        member = member + jnp.where(hit, 1.0, 0.0)
    earlier = lax.broadcasted_iota(jnp.int32, (rows, rows), 1) < lax.broadcasted_iota(
        jnp.int32, (rows, rows), 0
    )
    before = jnp.dot(
        jnp.where(earlier, 1.0, 0.0).astype(jnp.bfloat16),
        member.astype(jnp.bfloat16),
        preferred_element_type=jnp.float32,
    )
    slot = jnp.where(member > 0.0, before, -1.0)
    leading = weights.astype(jnp.bfloat16).astype(jnp.float32)
    table = jnp.where(field == 0, slot, jnp.where(field == 1, leading, weights - leading))
    table = table.astype(jnp.bfloat16)
    for relative in range(ranks):
        start = pl.multiple_of((place_ref[0] ^ relative) * part, 128)
        out_ref[relative, :, :part] = normed_ref[:, pl.ds(start, part)]
        out_ref[relative, :, part:] = table


def prepare_tokens(place, inputs, gain, ids, probs, ranks):
    rows, width = inputs.shape
    whole = pl.BlockSpec(memory_space=pltpu.VMEM)
    return call(
        functools.partial(prepare_kernel, ranks),
        "prepare_tokens",
        8 * inputs.size,
        4 * inputs.size,
        in_specs=[SMEM, whole, whole, whole, whole],
        out_specs=whole,
        out_shape=jax.ShapeDtypeStruct((ranks, rows, width // ranks + LANES), jnp.bfloat16),
        scratch_shapes=[pltpu.VMEM((rows, width), jnp.bfloat16)],
    )(place, inputs, gain, ids, probs)


def products_kernel(ranks, place_ref, tokens_ref, kept_ref, sent_ref, keep_ref, send_ref, table_ref):
    expert = pl.program_id(0)
    count = tokens_ref.shape[0]
    part = kept_ref.shape[1]

    @pl.when(expert == 0)
    def _():
        table_ref[...] = jnp.transpose(tokens_ref[:, part:].astype(jnp.float32))

    slot = table_ref[pl.ds(place_ref[1] * pl.num_programs(0) + expert, 1), :]
    token = lax.broadcasted_iota(jnp.int32, (1, count), 1)
    block = lax.bitwise_xor(lax.div(token, count // ranks), place_ref[0])
    row = jnp.where(slot >= 0.0, slot + (block * CAP).astype(jnp.float32), -1.0)
    number = lax.broadcasted_iota(jnp.int32, (ranks * CAP, count), 0).astype(jnp.float32)
    pick = jnp.where(row == number, 1.0, 0.0).astype(jnp.bfloat16)
    rows = jnp.dot(pick, tokens_ref[:, :part], preferred_element_type=jnp.float32)
    rows = rows.astype(jnp.bfloat16)
    send_ref[0] = jnp.dot(rows, sent_ref[0], preferred_element_type=jnp.float32).astype(jnp.bfloat16)
    keep_ref[0] = jnp.dot(rows, kept_ref[0], preferred_element_type=jnp.float32)


def products(place, tokens, weights, ranks):
    kept, sent = weights
    experts, part, columns = kept.shape
    rows = ranks * CAP
    weight_spec = pl.BlockSpec((1, part, columns), lambda e: (e, 0, 0))
    row_spec = pl.BlockSpec((1, rows, columns), lambda e: (e, 0, 0))
    return call(
        functools.partial(products_kernel, ranks),
        "products",
        2 * experts * rows * part * (2 * columns + tokens.shape[0]),
        4 * kept.size + 2 * tokens.size + 6 * experts * rows * columns,
        grid=(experts,),
        in_specs=[SMEM, pl.BlockSpec(tokens.shape, lambda e: (0, 0)), weight_spec, weight_spec],
        out_specs=[row_spec, row_spec],
        out_shape=[
            jax.ShapeDtypeStruct((experts, rows, columns), jnp.float32),
            jax.ShapeDtypeStruct((experts, rows, columns), jnp.bfloat16),
        ],
        scratch_shapes=[pltpu.VMEM((LANES, tokens.shape[0]), jnp.float32)],
    )(place, tokens, kept, sent)


def outputs_kernel(ranks, hidden, place_ref, table_ref, own_ref, other_ref, down_ref, keep_ref, send_ref, folded_ref):
    experts, rows, _ = own_ref.shape
    count = table_ref.shape[0]
    block_rows = count // ranks

    @pl.when(pl.program_id(0) == 0)
    def _():
        table = table_ref[...].astype(jnp.float32)
        lane = lax.broadcasted_iota(jnp.int32, table.shape, 1)
        token = lax.broadcasted_iota(jnp.int32, (count, 1), 0)
        block = lax.bitwise_xor(lax.div(token, block_rows), place_ref[0])
        offset = (block * CAP).astype(jnp.float32)
        number = lax.broadcasted_iota(jnp.int32, (count, rows), 1).astype(jnp.float32)
        for expert in range(experts):

            def column(field):
                wanted = field * EXPERTS + place_ref[1] * experts + expert
                return jnp.sum(jnp.where(lane == wanted, table, 0.0), axis=1, keepdims=True)

            slot = column(0)
            row = jnp.where(slot >= 0.0, slot + offset, -1.0)
            pick = jnp.where(row == number, 1.0, 0.0).astype(jnp.bfloat16)
            total = own_ref[expert] + other_ref[expert].astype(jnp.float32)
            gate, up = total[:, :hidden], total[:, hidden:]
            active = (gate / (1.0 + jnp.exp(-gate)) * up).astype(jnp.bfloat16)
            spread = jnp.dot(pick, active, preferred_element_type=jnp.float32)
            spread = spread * (column(1) + column(2))
            folded_ref[:, expert * hidden : (expert + 1) * hidden] = spread.astype(jnp.bfloat16)

    result = jnp.dot(folded_ref[...], down_ref[...], preferred_element_type=jnp.float32)
    half = ranks // 2
    for position, relative in enumerate(reversed_order(ranks)):
        piece = result[relative * block_rows : (relative + 1) * block_rows]
        start = (position % half) * block_rows
        if position < half:
            keep_ref[start : start + block_rows, :] = piece
        else:
            send_ref[start : start + block_rows, :] = piece.astype(jnp.bfloat16)


def outputs(place, tokens, own, other, down, ranks, hidden):
    count = tokens.shape[0]
    depth, width = down.shape
    tile = min(width, 1024)
    half_rows = count // 2
    out_spec = pl.BlockSpec((half_rows, tile), lambda j: (0, j))
    whole = pl.BlockSpec(own.shape, lambda j: (0, 0, 0))
    last = tokens.shape[1] // LANES - 1
    return call(
        functools.partial(outputs_kernel, ranks, hidden),
        "outputs",
        2 * count * depth * width,
        2 * down.size + 6 * own.size + 6 * half_rows * width,
        grid=(width // tile,),
        in_specs=[
            SMEM,
            pl.BlockSpec((count, LANES), lambda j: (0, last)),
            whole,
            whole,
            pl.BlockSpec((depth, tile), lambda j: (0, j)),
        ],
        out_specs=[out_spec, out_spec],
        out_shape=[
            jax.ShapeDtypeStruct((half_rows, width), jnp.float32),
            jax.ShapeDtypeStruct((half_rows, width), jnp.bfloat16),
        ],
        scratch_shapes=[pltpu.VMEM((count, depth), jnp.bfloat16)],
    )(place, tokens, own, other, down)


def per_device(
    fresh_tokens,
    in_flight,
    norm_weight,
    gate_up,
    down_proj,
    first_moment,
    second_moment,
    route_ids,
    route_probs,
    trade_flags,
):
    groups = lax.axis_size("expert")
    dp_ranks = lax.axis_size("dp")
    half_span = groups // 2
    top_bit = bits_of("expert") - 1
    own_rank = lax.axis_index("expert")
    dp_rank = lax.axis_index("dp")
    section_index = lax.axis_index("section")
    experts_here = gate_up.shape[1]
    hidden = down_proj.shape[2]
    width = fresh_tokens.shape[2]

    holdings = (gate_up, down_proj, first_moment, second_moment)
    counts = jnp.sum(trade_flags, axis=1)
    order = jnp.argsort(-trade_flags, axis=1, stable=True).astype(jnp.int32)
    own_pair = own_rank % half_span
    own_order = order[own_pair]
    own_count = counts[own_pair]

    def pair_route(pairs):
        return [(i, i ^ (1 << top_bit)) for i in range(groups) if i % half_span in pairs]

    def trade_round(moved, turn, pairs, beside_layers=False):
        slot = own_order[turn]
        active = turn < own_count
        if len(pairs) < half_span:
            active = jnp.logical_and(active, own_pair == pairs[0])
        sent = [lax.dynamic_slice_in_dim(array, slot, 1, axis=1) for array in holdings]
        if beside_layers:
            ranks = [[i, i + half_span] for i in range(half_span)]
            both = [lax.all_gather(array, "expert", axis_index_groups=ranks) for array in sent]
            other = 1 - own_rank // half_span
            arrived = [lax.dynamic_index_in_dim(array, other, 0, keepdims=False) for array in both]
        else:
            arrived = [lax.ppermute(array, "expert", pair_route(pairs)) for array in sent]
        return tuple(
            lax.dynamic_update_slice_in_dim(old, jnp.where(active, new, own), slot, axis=1)
            for old, new, own in zip(moved, arrived, sent)
        )

    moved = trade_round(
        holdings, jnp.int32(0), tuple(range(half_span)), beside_layers=True
    )

    place = jnp.stack([dp_rank, own_rank]).astype(jnp.int32)
    weights = arrange_weights(place, gate_up, dp_ranks, hidden)
    down_flat = down_proj[0].reshape(experts_here * hidden, width)

    def halve(kept, sent, axis, split_axis):
        for bit in range(bits_of(axis)):
            arrived = swap(sent, axis, bit)
            if bit == bits_of(axis) - 1:
                return kept, arrived
            total = kept + arrived.astype(jnp.float32)
            kept, sent = jnp.split(total, 2, axis=split_axis)
            sent = sent.astype(jnp.bfloat16)

    def layer(inputs, tick):
        prepared = prepare_tokens(
            place, inputs, norm_weight, route_ids[0, tick], route_probs[0, tick], dp_ranks
        )
        arrived = [prepared[0]] + [
            lax.ppermute(prepared[r], "dp", [(i, i ^ r) for i in range(dp_ranks)])
            for r in range(1, dp_ranks)
        ]
        tokens = [jnp.concatenate(arrived, axis=0)]
        for relative in range(1, groups):
            lowest = (relative & -relative).bit_length() - 1
            tokens.append(swap(tokens[relative ^ (1 << lowest)], "expert", lowest))
        partial = []
        for chunk in tokens:
            keep, send = products(place, chunk, weights, dp_ranks)
            own, other = halve(keep, send, "dp", 2)
            keep, send = outputs(place, chunk, own, other, down_flat, dp_ranks, hidden)
            own, other = halve(keep, send, "dp", 0)
            partial.append(own + other.astype(jnp.float32))
        for bit in range(bits_of("expert")):
            for relative in reversed(range(groups)):
                if relative & -relative == 1 << bit:
                    other = swap(partial[relative].astype(jnp.bfloat16), "expert", bit)
                    partial[relative ^ (1 << bit)] += other.astype(jnp.float32)
        return (inputs.astype(jnp.float32) + partial[0]).astype(jnp.bfloat16)

    sections = lax.axis_size("section")
    onward = [(i, i + 1) for i in range(sections - 1)]
    first_input = jnp.where(section_index == 0, fresh_tokens[0], in_flight)
    tick_zero = layer(first_input, 0)
    second_input = jnp.where(
        section_index == 0, fresh_tokens[1], lax.ppermute(tick_zero, "section", onward)
    )
    tick_one = layer(second_input, 1)
    layer_out = jnp.stack([tick_zero, tick_one])[None]

    if experts_here > 1:
        moved, layer_out = lax.optimization_barrier((moved, layer_out))
        fewest = jnp.min(counts)
        everyone = tuple(range(half_span))
        moved = lax.fori_loop(
            1, fewest, lambda turn, held: trade_round(held, turn, everyone), moved
        )
        start = jnp.maximum(fewest, 1)
        for pair in range(half_span):
            moved = lax.fori_loop(
                start,
                counts[pair],
                lambda turn, held, pair=pair: trade_round(held, turn, (pair,)),
                moved,
            )
    return (layer_out,) + tuple(moved)


def solution(mesh):
    return jax.shard_map(
        per_device,
        mesh=mesh,
        in_specs=(
            P(None, ("expert", "dp"), None),
            P(("expert", "dp"), None),
            P("section", None),
            P("section", "expert", None, "dp", None),
            P("section", "expert", "dp", None),
            P("section", "expert", "dp", None),
            P("section", "expert", "dp", None),
            P("section", None, ("expert", "dp"), None),
            P("section", None, ("expert", "dp"), None),
            P(),
        ),
        out_specs=(
            P("section", None, ("expert", "dp"), None),
            P("section", "expert", None, "dp", None),
            P("section", "expert", "dp", None),
            P("section", "expert", "dp", None),
            P("section", "expert", "dp", None),
        ),
        check_vma=False,
    )
```

```python
import functools

import jax
import jax.numpy as jnp
from jax import lax
from jax.experimental import pallas as pl
from jax.experimental.pallas import tpu as pltpu
from jax.sharding import PartitionSpec as P

EXPERTS = 16
CAP = 36
LANES = 128
VMEM_LIMIT = 24 * 1024 * 1024
SMEM = pl.BlockSpec(memory_space=pltpu.SMEM)


def swap(value, axis, bit):
    return lax.ppermute(value, axis, [(i, i ^ (1 << bit)) for i in range(lax.axis_size(axis))])


def bits_of(axis):
    return lax.axis_size(axis).bit_length() - 1


def reversed_order(count):
    if count == 1:
        return [0]
    return [2 * i for i in reversed_order(count // 2)] + [2 * i + 1 for i in reversed_order(count // 2)]


def call(kernel, name, flops, bytes_accessed, **options):
    return pl.pallas_call(
        kernel,
        name=name,
        cost_estimate=pl.CostEstimate(
            flops=flops, bytes_accessed=bytes_accessed, transcendentals=0
        ),
        compiler_params=pltpu.CompilerParams(vmem_limit_bytes=VMEM_LIMIT),
        **options,
    )


def arrange_kernel(ranks, hidden, place_ref, gate_up_ref, kept_ref, sent_ref):
    half = ranks // 2
    for rank in range(ranks):

        @pl.when(place_ref[0] == rank)
        def _():
            for position, relative in enumerate(reversed_order(ranks)):
                out_ref = kept_ref if position < half else sent_ref
                start = (position % half) * 2 * hidden
                columns = pl.ds((rank ^ relative) * hidden, hidden)
                out_ref[0, :, start : start + 2 * hidden] = jnp.concatenate(
                    [gate_up_ref[0, 0, 0, :, columns], gate_up_ref[0, 0, 1, :, columns]], axis=-1
                )


def arrange_weights(place, gate_up, ranks, hidden):
    _, experts, _, depth, columns = gate_up.shape
    tile = min(depth, 256)
    shape = jax.ShapeDtypeStruct((experts, depth, columns), jnp.bfloat16)
    spec = pl.BlockSpec((1, tile, columns), lambda e, d: (e, d, 0))
    return call(
        functools.partial(arrange_kernel, ranks, hidden),
        "arrange_weights",
        0,
        4 * gate_up.size,
        grid=(experts, depth // tile),
        in_specs=[SMEM, pl.BlockSpec((1, 1, 2, tile, columns), lambda e, d: (0, e, 0, d, 0))],
        out_specs=[spec, spec],
        out_shape=[shape, shape],
    )(place, gate_up)


def prepare_kernel(ranks, place_ref, inputs_ref, gain_ref, ids_ref, probs_ref, out_ref, normed_ref):
    rows, width = inputs_ref.shape
    part = width // ranks
    values = inputs_ref[...].astype(jnp.float32)
    inverse_rms = lax.rsqrt(jnp.mean(values * values, axis=-1, keepdims=True) + 1e-06)
    normed_ref[...] = (values * inverse_rms * gain_ref[...]).astype(jnp.bfloat16)

    probs = probs_ref[...]
    mix_weight = probs / jnp.sum(probs, axis=-1, keepdims=True)
    lane = lax.broadcasted_iota(jnp.int32, (rows, LANES), 1)
    field = lax.div(lane, EXPERTS)
    expert = lane - field * EXPERTS
    weights = jnp.zeros((rows, LANES), jnp.float32)
    member = jnp.zeros((rows, LANES), jnp.float32)
    for choice in range(probs.shape[1]):
        hit = ids_ref[:, choice : choice + 1] == expert
        weights = weights + jnp.where(hit, mix_weight[:, choice : choice + 1], 0.0)
        member = member + jnp.where(hit, 1.0, 0.0)
    earlier = lax.broadcasted_iota(jnp.int32, (rows, rows), 1) < lax.broadcasted_iota(
        jnp.int32, (rows, rows), 0
    )
    before = jnp.dot(
        jnp.where(earlier, 1.0, 0.0).astype(jnp.bfloat16),
        member.astype(jnp.bfloat16),
        preferred_element_type=jnp.float32,
    )
    slot = jnp.where(member > 0.0, before, -1.0)
    leading = weights.astype(jnp.bfloat16).astype(jnp.float32)
    table = jnp.where(field == 0, slot, jnp.where(field == 1, leading, weights - leading))
    table = table.astype(jnp.bfloat16)
    for relative in range(ranks):
        start = pl.multiple_of((place_ref[0] ^ relative) * part, 128)
        out_ref[relative, :, :part] = normed_ref[:, pl.ds(start, part)]
        out_ref[relative, :, part:] = table


def prepare_tokens(place, inputs, gain, ids, probs, ranks):
    rows, width = inputs.shape
    whole = pl.BlockSpec(memory_space=pltpu.VMEM)
    return call(
        functools.partial(prepare_kernel, ranks),
        "prepare_tokens",
        8 * inputs.size,
        4 * inputs.size,
        in_specs=[SMEM, whole, whole, whole, whole],
        out_specs=whole,
        out_shape=jax.ShapeDtypeStruct((ranks, rows, width // ranks + LANES), jnp.bfloat16),
        scratch_shapes=[pltpu.VMEM((rows, width), jnp.bfloat16)],
    )(place, inputs, gain, ids, probs)


def products_kernel(ranks, place_ref, tokens_ref, kept_ref, sent_ref, keep_ref, send_ref, table_ref):
    expert = pl.program_id(0)
    count = tokens_ref.shape[0]
    part = kept_ref.shape[1]

    @pl.when(expert == 0)
    def _():
        table_ref[...] = jnp.transpose(tokens_ref[:, part:].astype(jnp.float32))

    slot = table_ref[pl.ds(place_ref[1] * pl.num_programs(0) + expert, 1), :]
    token = lax.broadcasted_iota(jnp.int32, (1, count), 1)
    block = lax.bitwise_xor(lax.div(token, count // ranks), place_ref[0])
    row = jnp.where(slot >= 0.0, slot + (block * CAP).astype(jnp.float32), -1.0)
    number = lax.broadcasted_iota(jnp.int32, (ranks * CAP, count), 0).astype(jnp.float32)
    pick = jnp.where(row == number, 1.0, 0.0).astype(jnp.bfloat16)
    rows = jnp.dot(pick, tokens_ref[:, :part], preferred_element_type=jnp.float32)
    rows = rows.astype(jnp.bfloat16)
    send_ref[0] = jnp.dot(rows, sent_ref[0], preferred_element_type=jnp.float32).astype(jnp.bfloat16)
    keep_ref[0] = jnp.dot(rows, kept_ref[0], preferred_element_type=jnp.float32)


def products(place, tokens, weights, ranks):
    kept, sent = weights
    experts, part, columns = kept.shape
    rows = ranks * CAP
    weight_spec = pl.BlockSpec((1, part, columns), lambda e: (e, 0, 0))
    row_spec = pl.BlockSpec((1, rows, columns), lambda e: (e, 0, 0))
    return call(
        functools.partial(products_kernel, ranks),
        "products",
        2 * experts * rows * part * (2 * columns + tokens.shape[0]),
        4 * kept.size + 2 * tokens.size + 6 * experts * rows * columns,
        grid=(experts,),
        in_specs=[SMEM, pl.BlockSpec(tokens.shape, lambda e: (0, 0)), weight_spec, weight_spec],
        out_specs=[row_spec, row_spec],
        out_shape=[
            jax.ShapeDtypeStruct((experts, rows, columns), jnp.float32),
            jax.ShapeDtypeStruct((experts, rows, columns), jnp.bfloat16),
        ],
        scratch_shapes=[pltpu.VMEM((LANES, tokens.shape[0]), jnp.float32)],
    )(place, tokens, kept, sent)


def outputs_kernel(ranks, hidden, place_ref, table_ref, own_ref, other_ref, down_ref, keep_ref, send_ref, folded_ref):
    experts, rows, _ = own_ref.shape
    count = table_ref.shape[0]
    block_rows = count // ranks

    @pl.when(pl.program_id(0) == 0)
    def _():
        table = table_ref[...].astype(jnp.float32)
        lane = lax.broadcasted_iota(jnp.int32, table.shape, 1)
        token = lax.broadcasted_iota(jnp.int32, (count, 1), 0)
        block = lax.bitwise_xor(lax.div(token, block_rows), place_ref[0])
        offset = (block * CAP).astype(jnp.float32)
        number = lax.broadcasted_iota(jnp.int32, (count, rows), 1).astype(jnp.float32)
        for expert in range(experts):

            def column(field):
                wanted = field * EXPERTS + place_ref[1] * experts + expert
                return jnp.sum(jnp.where(lane == wanted, table, 0.0), axis=1, keepdims=True)

            slot = column(0)
            row = jnp.where(slot >= 0.0, slot + offset, -1.0)
            pick = jnp.where(row == number, 1.0, 0.0).astype(jnp.bfloat16)
            total = own_ref[expert] + other_ref[expert].astype(jnp.float32)
            gate, up = total[:, :hidden], total[:, hidden:]
            active = (gate / (1.0 + jnp.exp(-gate)) * up).astype(jnp.bfloat16)
            spread = jnp.dot(pick, active, preferred_element_type=jnp.float32)
            spread = spread * (column(1) + column(2))
            folded_ref[:, expert * hidden : (expert + 1) * hidden] = spread.astype(jnp.bfloat16)

    result = jnp.dot(folded_ref[...], down_ref[...], preferred_element_type=jnp.float32)
    half = ranks // 2
    for position, relative in enumerate(reversed_order(ranks)):
        piece = result[relative * block_rows : (relative + 1) * block_rows]
        start = (position % half) * block_rows
        if position < half:
            keep_ref[start : start + block_rows, :] = piece
        else:
            send_ref[start : start + block_rows, :] = piece.astype(jnp.bfloat16)


def outputs(place, tokens, own, other, down, ranks, hidden):
    count = tokens.shape[0]
    depth, width = down.shape
    tile = min(width, 1024)
    half_rows = count // 2
    out_spec = pl.BlockSpec((half_rows, tile), lambda j: (0, j))
    whole = pl.BlockSpec(own.shape, lambda j: (0, 0, 0))
    last = tokens.shape[1] // LANES - 1
    return call(
        functools.partial(outputs_kernel, ranks, hidden),
        "outputs",
        2 * count * depth * width,
        2 * down.size + 6 * own.size + 6 * half_rows * width,
        grid=(width // tile,),
        in_specs=[
            SMEM,
            pl.BlockSpec((count, LANES), lambda j: (0, last)),
            whole,
            whole,
            pl.BlockSpec((depth, tile), lambda j: (0, j)),
        ],
        out_specs=[out_spec, out_spec],
        out_shape=[
            jax.ShapeDtypeStruct((half_rows, width), jnp.float32),
            jax.ShapeDtypeStruct((half_rows, width), jnp.bfloat16),
        ],
        scratch_shapes=[pltpu.VMEM((count, depth), jnp.bfloat16)],
    )(place, tokens, own, other, down)


def per_device(
    fresh_tokens,
    in_flight,
    norm_weight,
    gate_up,
    down_proj,
    first_moment,
    second_moment,
    route_ids,
    route_probs,
    trade_flags,
):
    groups = lax.axis_size("expert")
    dp_ranks = lax.axis_size("dp")
    half_span = groups // 2
    top_bit = bits_of("expert") - 1
    own_rank = lax.axis_index("expert")
    dp_rank = lax.axis_index("dp")
    section_index = lax.axis_index("section")
    experts_here = gate_up.shape[1]
    hidden = down_proj.shape[2]
    width = fresh_tokens.shape[2]

    holdings = (gate_up, down_proj, first_moment, second_moment)
    counts = jnp.sum(trade_flags, axis=1)
    order = jnp.argsort(-trade_flags, axis=1, stable=True).astype(jnp.int32)
    own_pair = own_rank % half_span
    own_order = order[own_pair]
    own_count = counts[own_pair]

    def pair_route(pairs):
        return [(i, i ^ (1 << top_bit)) for i in range(groups) if i % half_span in pairs]

    def trade_round(moved, turn, pairs, beside_layers=False):
        slot = own_order[turn]
        active = turn < own_count
        if len(pairs) < half_span:
            active = jnp.logical_and(active, own_pair == pairs[0])
        sent = [lax.dynamic_slice_in_dim(array, slot, 1, axis=1) for array in holdings]
        if beside_layers:
            ranks = [[i, i + half_span] for i in range(half_span)]
            other = 1 - own_rank // half_span

            def gathered(arrays):
                joined = jnp.concatenate(arrays, axis=0) if len(arrays) > 1 else arrays[0]
                both = lax.all_gather(joined, "expert", axis_index_groups=ranks)
                mine = lax.dynamic_index_in_dim(both, other, 0, keepdims=False)
                return [mine[i : i + 1] for i in range(len(arrays))]

            arrived = gathered(sent[:1]) + gathered(sent[1:])
        else:
            arrived = [lax.ppermute(array, "expert", pair_route(pairs)) for array in sent]
        return tuple(
            lax.dynamic_update_slice_in_dim(old, jnp.where(active, new, own), slot, axis=1)
            for old, new, own in zip(moved, arrived, sent)
        )

    moved = trade_round(
        holdings, jnp.int32(0), tuple(range(half_span)), beside_layers=True
    )

    place = jnp.stack([dp_rank, own_rank]).astype(jnp.int32)
    weights = arrange_weights(place, gate_up, dp_ranks, hidden)
    down_flat = down_proj[0].reshape(experts_here * hidden, width)

    def halve(kept, sent, axis, split_axis):
        for bit in range(bits_of(axis)):
            arrived = swap(sent, axis, bit)
            if bit == bits_of(axis) - 1:
                return kept, arrived
            total = kept + arrived.astype(jnp.float32)
            kept, sent = jnp.split(total, 2, axis=split_axis)
            sent = sent.astype(jnp.bfloat16)

    def layer(inputs, tick):
        prepared = prepare_tokens(
            place, inputs, norm_weight, route_ids[0, tick], route_probs[0, tick], dp_ranks
        )
        arrived = [prepared[0]] + [
            lax.ppermute(prepared[r], "dp", [(i, i ^ r) for i in range(dp_ranks)])
            for r in range(1, dp_ranks)
        ]
        tokens = [jnp.concatenate(arrived, axis=0)]
        for relative in range(1, groups):
            lowest = (relative & -relative).bit_length() - 1
            tokens.append(swap(tokens[relative ^ (1 << lowest)], "expert", lowest))
        partial = []
        for chunk in tokens:
            keep, send = products(place, chunk, weights, dp_ranks)
            own, other = halve(keep, send, "dp", 2)
            keep, send = outputs(place, chunk, own, other, down_flat, dp_ranks, hidden)
            own, other = halve(keep, send, "dp", 0)
            partial.append(own + other.astype(jnp.float32))
        for bit in range(bits_of("expert")):
            for relative in reversed(range(groups)):
                if relative & -relative == 1 << bit:
                    other = swap(partial[relative].astype(jnp.bfloat16), "expert", bit)
                    partial[relative ^ (1 << bit)] += other.astype(jnp.float32)
        return (inputs.astype(jnp.float32) + partial[0]).astype(jnp.bfloat16)

    sections = lax.axis_size("section")
    onward = [(i, i + 1) for i in range(sections - 1)]
    first_input = jnp.where(section_index == 0, fresh_tokens[0], in_flight)
    tick_zero = layer(first_input, 0)
    second_input = jnp.where(
        section_index == 0, fresh_tokens[1], lax.ppermute(tick_zero, "section", onward)
    )
    tick_one = layer(second_input, 1)
    layer_out = jnp.stack([tick_zero, tick_one])[None]

    if experts_here > 1:
        moved, layer_out = lax.optimization_barrier((moved, layer_out))
        fewest = jnp.min(counts)
        everyone = tuple(range(half_span))
        moved = lax.fori_loop(
            1, fewest, lambda turn, held: trade_round(held, turn, everyone), moved
        )
        start = jnp.maximum(fewest, 1)
        for pair in range(half_span):
            moved = lax.fori_loop(
                start,
                counts[pair],
                lambda turn, held, pair=pair: trade_round(held, turn, (pair,)),
                moved,
            )
    return (layer_out,) + tuple(moved)


def solution(mesh):
    return jax.shard_map(
        per_device,
        mesh=mesh,
        in_specs=(
            P(None, ("expert", "dp"), None),
            P(("expert", "dp"), None),
            P("section", None),
            P("section", "expert", None, "dp", None),
            P("section", "expert", "dp", None),
            P("section", "expert", "dp", None),
            P("section", "expert", "dp", None),
            P("section", None, ("expert", "dp"), None),
            P("section", None, ("expert", "dp"), None),
            P(),
        ),
        out_specs=(
            P("section", None, ("expert", "dp"), None),
            P("section", "expert", None, "dp", None),
            P("section", "expert", "dp", None),
            P("section", "expert", "dp", None),
            P("section", "expert", "dp", None),
        ),
        check_vma=False,
    )
```
